32 devices in a mesh: clips: 2 (over y), tiles: 4 (over z), tensor: 4 (over x, core).
Axes of the slice: x: 2, y: 2, z: 4, core: 2. Of those that a mesh axis runs over, the one named last changes fastest.
Arguments:
- attn_inputs: bfloat16 [3, 32, 4, 32, 3072], P(None, 'clips', None, 'tiles', 'tensor'), parts along dimension 1, may hold values from -64 to 64
- cell_valid: int32 [32, 4, 32], P('clips', None, 'tiles'), parts along dimension 0, may hold values from 0 to 1, as said below
- window_shift: int32 [2], replicated, may hold values from 1 to 7, as said below
- out_weight: bfloat16 [3072, 3072], P('tensor', 'tiles'), may hold values from -0.109375 to 0.109375
- cotangent: bfloat16 [16, 8, 32, 3072], P('tensor', 'clips', 'tiles'), parts along dimension 1, may hold values from -6 to 6
Outputs:
- layer_out: bfloat16 [16, 8, 32, 3072], P('tensor', 'clips', 'tiles'), parts along dimension 1
- grad_inputs: bfloat16 [3, 32, 4, 32, 3072], P(None, 'clips', None, 'tiles', 'tensor'), parts along dimension 1
The draws below stay inside these ranges and needn't reach their ends.
There are 2 independent parts, one for each index of `clips`. The reference program is written for one: setup_inputs(seed, part) draws one part's arguments, and reference() takes and returns one part's arrays. A program takes and returns all parts, laid end to end along the dimension named above; an argument that names none is the same for every part. Nothing has to cross between parts.
Inputs may be any that keep to these rules, and one draw needn't show every extreme that they name: `cell_valid`: every cell is valid at frame 0, and along frames the valid ones come first. `window_shift`: one offset is 1 and the other is 7, in either order.
All inputs are finite; a program needn't handle non-finite values.
Results may differ from the reference program's by a relative error of at most 0.018.
Values may be sent and summed in bfloat16 or wider, within the bound.
A program may use at most 64 MiB of HBM per device.

```python
import math
import jax
import jax.numpy as jnp
from jax import lax

D = 3072
HEADS = 24
HEAD_DIM = 128
WIN = 8
NT = 4
NW = 16
NH = 32
N_TENSOR = 4


def draw_attn_inputs(key, part):
    key = jax.random.fold_in(key, 11)
    arr_shape = (3, NW, NT, NH, HEADS * HEAD_DIM)
    base_key = jax.random.fold_in(key, 0)
    result = jnp.clip(jax.random.normal(base_key, arr_shape, jnp.float32), -6.0, 6.0)
    return result.astype(jnp.bfloat16)


def draw_cell_valid(key, part):
    key = jax.random.fold_in(key, 12)
    frame_limit = jax.random.randint(key, (NW, 1, NH), 1, NT + 1)
    return (jnp.arange(NT)[None, :, None] < frame_limit).astype(jnp.int32)


def draw_window_shift(key, part):
    key = jax.random.fold_in(key, 13)
    flipped = jax.random.randint(key, (), 0, 2)
    first_shift = 1 + (WIN - 2) * flipped
    return jnp.stack([first_shift, WIN - first_shift]).astype(jnp.int32)


def shard_levels(rng, shape, shards, smallest, largest):
    level = 1.0
    for axis_at, blocks in shards:
        draws = jax.random.uniform(jax.random.fold_in(jax.random.fold_in(rng, 6), axis_at), (blocks,), jnp.float32, smallest / len(shards), largest / len(shards))
        level = level * jnp.repeat(jnp.exp(draws), shape[axis_at] // blocks).reshape((-1,) + (1,) * (len(shape) - 1 - axis_at))
    return level


def noise(key, extent, deviation, bound, cuts=(), kind=jnp.bfloat16):
    drawn = jax.random.normal(key, extent, jnp.float32) * deviation
    if len(cuts) > 0:
        drawn = shard_levels(key, extent, cuts, -0.22, 0.18) * drawn
    return jnp.clip(drawn, min=-bound, max=bound).astype(kind)


def setup_inputs(seed: int = 0, part: int = 0) -> dict:
    seeds = jax.random.split(jax.random.key(seed), 6)
    part_keys = jax.random.split(jax.random.fold_in(seeds[5], part), 6)
    return {
        "attn_inputs": draw_attn_inputs(jax.random.fold_in(jax.random.fold_in(seeds[5], part), 71), part),
        "cell_valid": draw_cell_valid(jax.random.fold_in(jax.random.fold_in(seeds[5], part), 71), part),
        "window_shift": draw_window_shift(jax.random.fold_in(seeds[5], 71), part),
        "out_weight": noise(seeds[3], (HEADS * HEAD_DIM, D), (HEADS * HEAD_DIM) ** -0.5, 0.109375, ((0, 4), (1, 4))),
        "cotangent": noise(part_keys[4], (NW, NT, NH, D), 1.0, 6.0, ((0, 4), (2, 4))),
    }


def window_view(source, win_side):
    col_count, frame_count, row_count, chan_count = source.shape
    blocks = source.reshape(col_count // win_side, win_side, frame_count, row_count // win_side, win_side, chan_count)
    blocks = blocks.transpose(0, 3, 1, 2, 4, 5)
    return blocks.reshape(col_count // win_side * (row_count // win_side), win_side * frame_count * win_side, chan_count)

def window_unview(blocks, col_count, frame_count, row_count, win_side):
    chan_count = blocks.shape[-1]
    grid = blocks.reshape(col_count // win_side, row_count // win_side, win_side, frame_count, win_side, chan_count)
    grid = grid.transpose(0, 2, 3, 1, 4, 5)
    return grid.reshape(col_count, frame_count, row_count, chan_count)

def reference(attn_inputs, cell_valid, window_shift, out_weight, cotangent):
    row_shift = window_shift[0]
    col_shift = window_shift[1]
    att_scale = 1.0 / math.sqrt(HEAD_DIM)
    width_all = HEADS * HEAD_DIM
    rolled = jnp.roll(jnp.roll(attn_inputs, -row_shift, axis=3), -col_shift, axis=1)
    keep_grid = jnp.roll(jnp.roll(cell_valid, -row_shift, axis=2), -col_shift, axis=0)
    row_flag = (jnp.arange(NH) >= NH - row_shift).astype(jnp.int32)
    col_flag = (jnp.arange(NW) >= NW - col_shift).astype(jnp.int32)
    region = jnp.broadcast_to(2 * row_flag[None, None, :] + col_flag[:, None, None], (NW, NT, NH))
    win_region = window_view(region[..., None], WIN)[..., 0]
    win_keep = window_view(keep_grid[..., None], WIN)[..., 0]
    allowed = (win_region[:, :, None] == win_region[:, None, :]) & (win_keep[:, None, :] > 0)
    grad_attended = jnp.dot(cotangent.reshape(-1, D), out_weight.T, preferred_element_type=jnp.float32)
    grad_attended = grad_attended.astype(jnp.bfloat16).reshape(NW, NT, NH, width_all)
    grad_rolled = jnp.roll(jnp.roll(grad_attended, -row_shift, axis=2), -col_shift, axis=0)

    def split_heads(source):
        blocks = window_view(source, WIN)
        return blocks.reshape(blocks.shape[0], blocks.shape[1], HEADS, HEAD_DIM).transpose(2, 0, 1, 3)

    def merge_heads(stacked):
        blocks = stacked.transpose(1, 2, 0, 3)
        blocks = blocks.reshape(blocks.shape[0], blocks.shape[1], width_all)
        grid = window_unview(blocks, NW, NT, NH, WIN)
        return jnp.roll(jnp.roll(grid, row_shift, axis=2), col_shift, axis=0)

    def one_head(operands):
        query, key_win, values, grad_out = operands
        query_f = query.astype(jnp.float32)
        key_f = key_win.astype(jnp.float32)
        value_f = values.astype(jnp.float32)
        grad_f = grad_out.astype(jnp.float32)
        scores = jnp.einsum('nqd,nkd->nqk', query_f, key_f) * att_scale
        scores = jnp.where(allowed, scores, -1e+30)
        row_max = lax.optimization_barrier(jnp.max(scores, axis=-1, keepdims=True))
        weights = jnp.exp(scores - row_max)
        probs = weights / lax.optimization_barrier(jnp.sum(weights, axis=-1, keepdims=True))
        probs_low = probs.astype(jnp.bfloat16)
        attended = jnp.einsum('nqk,nkd->nqd', probs_low.astype(jnp.float32), value_f).astype(jnp.bfloat16)
        row_total = lax.optimization_barrier(jnp.sum(grad_f * attended.astype(jnp.float32), axis=-1))
        grad_probs = jnp.einsum('nqd,nkd->nqk', grad_f, value_f)
        grad_scores = (probs * (grad_probs - row_total[..., None])).astype(jnp.bfloat16)
        grad_scores_f = grad_scores.astype(jnp.float32)
        grad_query = (jnp.einsum('nqk,nkd->nqd', grad_scores_f, key_f) * att_scale).astype(jnp.bfloat16)
        grad_key = (jnp.einsum('nqk,nqd->nkd', grad_scores_f, query_f) * att_scale).astype(jnp.bfloat16)
        grad_value = jnp.einsum('nqk,nqd->nkd', probs_low.astype(jnp.float32), grad_f).astype(jnp.bfloat16)
        return (attended, grad_query, grad_key, grad_value)
    outputs = lax.map(one_head, (split_heads(rolled[0]), split_heads(rolled[1]), split_heads(rolled[2]), split_heads(grad_rolled)))
    attended_grid = merge_heads(outputs[0])
    grad_inputs = jnp.stack([merge_heads(outputs[1]), merge_heads(outputs[2]), merge_heads(outputs[3])])
    group_width = width_all // N_TENSOR
    flat_attended = attended_grid.reshape(-1, N_TENSOR, group_width)
    weight_groups = out_weight.reshape(N_TENSOR, group_width, D)
    total = jnp.zeros((flat_attended.shape[0], D), jnp.float32)
    for group in range(N_TENSOR):
        partial_sum = jnp.dot(flat_attended[:, group], weight_groups[group], preferred_element_type=jnp.float32).astype(jnp.bfloat16)
        total = total + lax.optimization_barrier(partial_sum).astype(jnp.float32)
    layer_out = total.astype(jnp.bfloat16).reshape(NW, NT, NH, D)
    return (layer_out, grad_inputs)
```

```python
import functools
import math

import jax
import jax.numpy as jnp
from jax import lax
from jax.experimental import pallas as pl
from jax.experimental.pallas import tpu as pltpu
from jax.sharding import PartitionSpec as P

HEAD_DIM = 128


def from_behind(block, axis, distance):
    devices = range(lax.axis_size(axis))
    route = [((i - distance) % len(devices), i) for i in devices]
    return lax.ppermute(block, axis, route)


def window_view(source, win_side):
    col_count, frame_count, row_count, chan_count = source.shape
    blocks = source.reshape(
        col_count // win_side, win_side, frame_count, row_count // win_side, win_side, chan_count
    )
    blocks = blocks.transpose(0, 3, 1, 2, 4, 5)
    return blocks.reshape(
        col_count // win_side * (row_count // win_side),
        win_side * frame_count * win_side,
        chan_count,
    )


def window_unview(blocks, col_count, frame_count, row_count, win_side):
    chan_count = blocks.shape[-1]
    grid = blocks.reshape(
        col_count // win_side, row_count // win_side, win_side, frame_count, win_side, chan_count
    )
    grid = grid.transpose(0, 2, 3, 1, 4, 5)
    return grid.reshape(col_count, frame_count, row_count, chan_count)


def attend(query, key_win, values, region, keep_mask, att_scale):
    scores = (
        jnp.einsum("nqhd,nkhd->nhqk", query, key_win, preferred_element_type=jnp.float32)
        * att_scale
    )
    allowed = (region[:, None, :, None] == region[:, None, None, :]) & (
        keep_mask[:, None, None, :] > 0.5
    )
    scores = jnp.where(allowed, scores, -1e30)
    row_max = jnp.max(scores, axis=-1, keepdims=True)
    weights = jnp.exp(scores - row_max)
    probs = weights / jnp.sum(weights, axis=-1, keepdims=True)
    probs_low = probs.astype(jnp.bfloat16)
    attended = jnp.einsum(
        "nhqk,nkhd->nqhd", probs_low, values, preferred_element_type=jnp.float32
    ).astype(jnp.bfloat16)
    return (attended, probs, probs_low)


def attend_back(query, key_win, values, attended, probs, probs_low, grad_out, att_scale):
    row_total = jnp.sum(grad_out.astype(jnp.float32) * attended.astype(jnp.float32), axis=-1)
    grad_probs = jnp.einsum("nqhd,nkhd->nhqk", grad_out, values, preferred_element_type=jnp.float32)
    grad_scores = (probs * (grad_probs - jnp.transpose(row_total, (0, 2, 1))[..., None])).astype(
        jnp.bfloat16
    )
    grad_query = (
        jnp.einsum("nhqk,nkhd->nqhd", grad_scores, key_win, preferred_element_type=jnp.float32)
        * att_scale
    ).astype(jnp.bfloat16)
    grad_key = (
        jnp.einsum("nhqk,nqhd->nkhd", grad_scores, query, preferred_element_type=jnp.float32)
        * att_scale
    ).astype(jnp.bfloat16)
    grad_value = jnp.einsum(
        "nhqk,nqhd->nkhd", probs_low, grad_out, preferred_element_type=jnp.float32
    ).astype(jnp.bfloat16)
    return (grad_query, grad_key, grad_value)


def shifted(row_shift, col_shift, attn_inputs, valid_low, out_weight, cotangent):
    win_side = attn_inputs.shape[3]
    full_width = attn_inputs.shape[1]
    frame_count = attn_inputs.shape[2]
    chan_count = attn_inputs.shape[4]
    head_count = chan_count // HEAD_DIM
    att_scale = 1.0 / math.sqrt(HEAD_DIM)
    early = row_shift * 2 < win_side
    slot = 0 if early else win_side - 1
    step = -1 if early else 1
    tile_index = lax.axis_index("tiles")
    wraps = tile_index == (lax.axis_size("tiles") - 1 if early else 0)
    in_slot = jnp.arange(win_side) == slot

    def take(block, distance):
        band = block[..., slot : slot + 1, :]
        moved = from_behind(band, "tiles", distance)
        return jnp.where(in_slot[:, None], moved, block)

    win_inputs = jnp.roll(take(attn_inputs, step), -col_shift, axis=1)
    win_valid = jnp.roll(take(valid_low[..., None], step)[..., 0], -col_shift, axis=0)
    row_flag = (wraps & in_slot).astype(jnp.int32)
    col_flag = (jnp.arange(full_width) >= full_width - col_shift).astype(jnp.int32)
    region_grid = jnp.broadcast_to(
        2 * row_flag[None, None, :] + col_flag[:, None, None], (full_width, frame_count, win_side)
    )
    win_region = window_view(region_grid[..., None], win_side)[..., 0]
    win_keep = window_view(win_valid[..., None], win_side)[..., 0]

    def to_heads(source):
        blocks = window_view(source, win_side)
        return blocks.reshape(blocks.shape[0], blocks.shape[1], head_count, HEAD_DIM)

    def from_heads(stacked):
        blocks = stacked.reshape(stacked.shape[0], stacked.shape[1], chan_count)
        grid = window_unview(blocks, full_width, frame_count, win_side, win_side)
        return jnp.roll(grid, col_shift, axis=0)

    columns = lax.all_gather(out_weight, "tiles", axis=1, tiled=True)
    all_cotangent = lax.all_gather(cotangent, "tensor", axis=0, tiled=True)
    query = to_heads(win_inputs[0])
    key_win = to_heads(win_inputs[1])
    values = to_heads(win_inputs[2])
    attended, probs, probs_low = attend(query, key_win, values, win_region, win_keep, att_scale)
    own_attended = take(from_heads(attended), -step)
    layer_out = lax.psum_scatter(
        jnp.einsum(
            "wtsf,fd->wtsd", own_attended, columns, preferred_element_type=jnp.float32
        ).astype(jnp.bfloat16),
        "tensor",
        scatter_dimension=0,
        tiled=True,
    )
    grad_attended = jnp.einsum(
        "wtsd,fd->wtsf", all_cotangent, columns, preferred_element_type=jnp.float32
    ).astype(jnp.bfloat16)
    win_grad = jnp.roll(take(grad_attended, step), -col_shift, axis=0)
    grads = attend_back(
        query, key_win, values, attended, probs, probs_low, to_heads(win_grad), att_scale
    )
    grad_rows = jnp.stack([from_heads(grad) for grad in grads])
    return (layer_out, take(grad_rows, -step))


NT_DIMS = (((1,), (1,)), ((), ()))
TN_DIMS = (((0,), (0,)), ((), ()))
NN_DIMS = (((1,), (0,)), ((), ()))
BF16 = jnp.bfloat16
F32 = jnp.float32


def mm(left, right, dims=NN_DIMS):
    return lax.dot_general(left, right, dims, preferred_element_type=F32)


def fused_kernel(
    early, col_shift, win_side, frames, tiles, tensors, clips,
    qkv, valid, weight, cot,
    out_ref, grad_ref,
    gathered, cots, band_out, band_in, valid_in, win_qkv, att, att_out, att_in, own_att,
    probs, biases, grad_half, grad_out, grad_in, grad_win, results, res_out, res_in, parts, shares,
    w_send, w_recv, f_send, f_recv, c_send, c_recv, b_send, b_recv, r_send, r_recv,
):
    cells, chans = qkv.shape[1], qkv.shape[2]
    heads = chans // HEAD_DIM
    half_heads = heads // 2
    half = chans // 2
    cols = weight.shape[1]
    share = cot.shape[0]
    bands = cells // win_side
    win = cells // 2
    roll = col_shift * frames * win_side
    scale = 1.0 / math.sqrt(HEAD_DIM)
    slot = 0 if early else win_side - 1
    step = -1 if early else 1
    z = lax.axis_index("tiles")
    t = lax.axis_index("tensor")
    c = lax.axis_index("clips")
    wraps = z == (tiles - 1 if early else 0)

    def tile(k):
        return {"tiles": lax.rem(z + (k % tiles), tiles)}

    def tensor(k):
        return {"tensor": lax.rem(t + (k % tensors), tensors)}

    partner = {"clips": 1 - c}

    def remote(src, dst, send, recv, device):
        return pltpu.make_async_remote_copy(
            src_ref=src, dst_ref=dst, send_sem=send, recv_sem=recv,
            device_id=device, device_id_type=pl.DeviceIdType.MESH,
        )

    barrier = pltpu.get_barrier_semaphore()
    peers = [tile(k) for k in range(1, tiles)] + [tensor(k) for k in range(1, tensors)] + [partner]
    for peer in peers:
        pl.semaphore_signal(barrier, inc=1, device_id=peer, device_id_type=pl.DeviceIdType.MESH)

    picks = lax.broadcasted_iota(jnp.int32, (bands, cells), 1)
    rows = lax.broadcasted_iota(jnp.int32, (bands, cells), 0)
    pick = (picks == rows * win_side + slot).astype(BF16)
    put_rows = lax.broadcasted_iota(jnp.int32, (cells, bands), 0)
    put_cols = lax.broadcasted_iota(jnp.int32, (cells, bands), 1)
    put = (put_rows == put_cols * win_side + slot).astype(BF16)

    def take(block):
        return mm(pick, block).astype(BF16)

    def merge(own, band):
        spread = mm(put, band)
        at = lax.rem(lax.broadcasted_iota(jnp.int32, spread.shape, 0), win_side) == slot
        return jnp.where(at, spread, own.astype(F32)).astype(BF16)

    def rolled(block):
        return jnp.concatenate([block[roll:], block[:roll]], axis=0)

    def unrolled(block):
        return jnp.concatenate([block[cells - roll:], block[: cells - roll]], axis=0)

    for i in range(3):
        band_out[pl.ds(i * bands, bands), :] = take(qkv[i])
    pl.semaphore_wait(barrier, len(peers))

    started = []

    def go(copy):
        copy.start()
        started.append(copy)
        return copy

    band_copy = go(remote(band_out, band_in, b_send.at[0], b_recv.at[0], tile(step)))
    valid_copy = go(remote(valid, valid_in, b_send.at[1], b_recv.at[1], tile(step)))
    cross = go(remote(cot, cots.at[1], c_send.at[0], c_recv.at[0], {"tensor": lax.rem(t + 2, 4)}))
    sib_id = {"tensor": t + 1 - 2 * lax.rem(t, 2)}
    sib = go(remote(cot, cots.at[0], c_send.at[1], c_recv.at[1], sib_id))
    mine = pl.ds(pl.multiple_of(c * half, half), half)
    theirs = pl.ds(pl.multiple_of((1 - c) * half, half), half)
    order = [1, tiles - 1] + [k for k in range(2, tiles - 1)]
    direct = {}
    for k in order:
        at = tiles - k - 1
        direct[tiles - k] = go(remote(
            weight.at[mine, :], gathered.at[at, mine, :], w_send.at[at], w_recv.at[at], tile(k)
        ))
    forward = {}

    def pass_on(k):
        direct[k].wait_recv()
        forward[k] = go(remote(
            gathered.at[k - 1, mine, :], gathered.at[k - 1, mine, :],
            f_send.at[k - 1], f_recv.at[k - 1], partner,
        ))

    band_copy.wait_recv()
    valid_copy.wait_recv()
    for i in range(3):
        for h in range(heads):
            lanes = pl.ds(h * HEAD_DIM, HEAD_DIM)
            win_qkv[i, h] = rolled(merge(qkv[i, :, lanes], band_in[pl.ds(i * bands, bands), lanes]))

    lane = lax.broadcasted_iota(jnp.int32, (8, cells), 1)
    keep = jnp.where(lax.rem(lane, win_side) == slot, valid_in[...], valid[...])
    spot_q = lax.broadcasted_iota(jnp.int32, (win, win), 0)
    spot_k = lax.broadcasted_iota(jnp.int32, (win, win), 1)
    wrap_flag = jnp.where(wraps, 2, 0)
    for w in range(2):
        edge = (win_side - col_shift) * frames * win_side

        def region(spot):
            row_flag = jnp.where(lax.rem(spot, win_side) == slot, wrap_flag, 0)
            return row_flag + (jnp.where(spot >= edge, 1, 0) if w == 1 else 0)

        allowed = (region(spot_q) == region(spot_k)) & (keep[0:1, w * win : (w + 1) * win] > 0.5)
        biases[w] = jnp.where(allowed, 0.0, -1e30)

    @pl.loop(0, heads)
    def _(h):
        for w in range(2):
            at = pl.ds(w * win, win)
            scores = mm(win_qkv[0, h, at], win_qkv[1, h, at], NT_DIMS) * scale + biases[w]
            row_max = jnp.max(scores, axis=-1, keepdims=True)
            weights = jnp.exp(scores - row_max)
            low = (weights / jnp.sum(weights, axis=-1, keepdims=True)).astype(BF16)
            probs[h, w] = low
            att[h, at] = mm(low, win_qkv[2, h, at]).astype(BF16)

    for h in range(heads):
        att_out[:, pl.ds(h * HEAD_DIM, HEAD_DIM)] = take(att[h])
    att_copy = go(remote(att_out, att_in, b_send.at[2], b_recv.at[2], tile(-step)))
    pass_on(1)

    cross.wait_recv()
    third = go(remote(cots.at[1], cots.at[2], c_send.at[2], c_recv.at[2], sib_id))
    sib.wait_recv()
    third.wait_recv()
    att_copy.wait_recv()
    for h in range(heads):
        lanes = pl.ds(h * HEAD_DIM, HEAD_DIM)
        own_att[:, lanes] = unrolled(merge(att[h], att_in[:, lanes]))

    def cot_block(j, cols_at):
        return cot[:, cols_at] if j == 0 else cots[j - 1, :, cols_at]

    flip = 1 - 2 * lax.rem(t, 2)
    owners = [t, t + flip, lax.rem(t + 2, 4), lax.rem(t + flip + 2, 4)]

    def w_rows(k, at):
        return weight[at, :] if k == 0 else gathered[k - 1, at, :]

    def back(k, which):
        at = mine if which == 0 else theirs
        cols_at = pl.ds(pl.multiple_of(lax.rem(z + k, tiles) * cols, cols), cols)
        for j in range(4):
            rows_at = pl.ds(pl.multiple_of(owners[j] * share, share), share)
            value = mm(cot_block(j, cols_at), w_rows(k, at), NT_DIMS)
            if k == 0:
                grad_half[which, rows_at] = value
            else:
                grad_half[which, rows_at] = grad_half[which, rows_at] + value

    def project(k):
        def block(u):
            rows_at = pl.ds(pl.multiple_of(u * share, share), share)
            return mm(own_att[rows_at], w_rows(k, slice(None))).astype(BF16)

        for j in range(1, 4):
            parts[k, j - 1] = block(owners[j])
            go(remote(
                parts.at[k, j - 1], shares.at[k, j - 1],
                r_send.at[k, j - 1], r_recv.at[k, j - 1], {"tensor": owners[j]},
            ))
        parts[k, 3] = block(t)

    first = [c * half_heads, (1 - c) * half_heads]
    grad_copies = {}

    def send_grad(which):
        grad_out[which] = take(grad_half[which].astype(BF16))
        grad_copies[which] = go(remote(
            grad_out.at[which], grad_in.at[which],
            b_send.at[3 + which], b_recv.at[3 + which], tile(step),
        ))

    result_copies = {}

    def attention_back(which):
        grad_copies[which].wait_recv()
        for j in range(half_heads):
            lanes = pl.ds(j * HEAD_DIM, HEAD_DIM)
            grad_win[which, j] = rolled(
                merge(grad_half[which, :, lanes].astype(BF16), grad_in[which, :, lanes])
            )

        @pl.loop(0, half_heads)
        def _(j):
            h = first[which] + j
            for w in range(2):
                at = pl.ds(w * win, win)
                grad = grad_win[which, j, at]
                low = probs[h, w]
                total = jnp.sum(
                    grad.astype(F32) * att[h, at].astype(F32), axis=-1, keepdims=True
                )
                grad_probs = mm(grad, win_qkv[2, h, at], NT_DIMS)
                grad_scores = (low.astype(F32) * (grad_probs - total)).astype(BF16)
                results[which, 0, j, at] = (mm(grad_scores, win_qkv[1, h, at]) * scale).astype(BF16)
                results[which, 1, j, at] = (
                    mm(grad_scores, win_qkv[0, h, at], TN_DIMS) * scale
                ).astype(BF16)
                results[which, 2, j, at] = mm(low, grad, TN_DIMS).astype(BF16)

        for i in range(3):
            for j in range(half_heads):
                res_out[which, i, :, pl.ds(j * HEAD_DIM, HEAD_DIM)] = take(results[which, i, j])
        result_copies[which] = go(remote(
            res_out.at[which], res_in.at[which],
            b_send.at[5 + which], b_recv.at[5 + which], tile(-step),
        ))

    def finish(which):
        result_copies[which].wait_recv()
        for i in range(3):
            for j in range(half_heads):
                lanes = pl.ds(pl.multiple_of((first[which] + j) * HEAD_DIM, HEAD_DIM), HEAD_DIM)
                own = unrolled(merge(
                    results[which, i, j], res_in[which, i, :, pl.ds(j * HEAD_DIM, HEAD_DIM)]
                ))
                grad_ref[i, :, lanes] = own

    back(0, 0)
    back(0, 1)
    project(0)
    for k in order[1:]:
        pass_on(k)
    for k in order:
        back(k, 0)
    send_grad(0)
    for n, k in enumerate(order):
        forward[k].wait_recv()
        back(k, 1)
        if k == order[-1]:
            send_grad(1)
        project(k)
        if n == 0:
            attention_back(0)
    attention_back(1)
    for k in range(tiles):
        cols_at = pl.ds(pl.multiple_of(lax.rem(z + k, tiles) * cols, cols), cols)
        total = parts[k, 3].astype(F32)
        for j in range(1, 4):
            remote(
                parts.at[k, j - 1], shares.at[k, j - 1],
                r_send.at[k, j - 1], r_recv.at[k, j - 1], {"tensor": owners[j]},
            ).wait_recv()
            total = total + shares[k, j - 1].astype(F32)
        out_ref[:, cols_at] = total.astype(BF16)
    finish(0)
    finish(1)
    for copy in started:
        copy.wait_send()


def fused(sizes, early, attn_inputs, cell_valid, out_weight, cotangent):
    tiles, tensors, clips = sizes
    _, columns, frames, win_side, chans = attn_inputs.shape
    col_shift = win_side - 1 if early else 1
    cells = columns * frames * win_side
    heads, half = chans // HEAD_DIM, chans // 2
    bands, win = cells // win_side, cells // 2
    share = cells // tensors
    cols = out_weight.shape[1]
    width = cotangent.shape[-1]
    flat_valid = jnp.roll(cell_valid, -col_shift, axis=0).astype(F32).reshape(1, cells)
    vmem = pltpu.VMEM
    dma = pltpu.SemaphoreType.DMA
    in_vmem = pl.BlockSpec(memory_space=pltpu.VMEM)
    layer_out, grads = pl.pallas_call(
        functools.partial(
            fused_kernel, early, col_shift, win_side, frames, tiles, tensors, clips
        ),
        out_shape=(
            jax.ShapeDtypeStruct((share, width), BF16),
            jax.ShapeDtypeStruct((3, cells, chans), BF16),
        ),
        in_specs=[in_vmem] * 4,
        out_specs=(in_vmem, in_vmem),
        scratch_shapes=[
            vmem((tiles - 1, chans, cols), BF16),
            vmem((3, share, width), BF16),
            vmem((3 * bands, chans), BF16),
            vmem((3 * bands, chans), BF16),
            vmem((8, cells), F32),
            vmem((3, heads, cells, HEAD_DIM), BF16),
            vmem((heads, cells, HEAD_DIM), BF16),
            vmem((bands, chans), BF16),
            vmem((bands, chans), BF16),
            vmem((cells, chans), BF16),
            vmem((heads, 2, win, win), BF16),
            vmem((2, win, win), F32),
            vmem((2, cells, half), F32),
            vmem((2, bands, half), BF16),
            vmem((2, bands, half), BF16),
            vmem((2, heads // 2, cells, HEAD_DIM), BF16),
            vmem((2, 3, heads // 2, cells, HEAD_DIM), BF16),
            vmem((2, 3, bands, half), BF16),
            vmem((2, 3, bands, half), BF16),
            vmem((tiles, 4, share, cols), BF16),
            vmem((tiles, 3, share, cols), BF16),
            dma((tiles - 1,)), dma((tiles - 1,)), dma((tiles - 1,)), dma((tiles - 1,)),
            dma((3,)), dma((3,)), dma((7,)), dma((7,)), dma((tiles, 3)), dma((tiles, 3)),
        ],
        compiler_params=pltpu.CompilerParams(
            collective_id=0 if early else 1,
            has_side_effects=True,
            vmem_limit_bytes=56 * 2**20,
        ),
        name="fused_early" if early else "fused_late",
    )(
        attn_inputs.reshape(3, cells, chans),
        jnp.broadcast_to(flat_valid, (8, cells)),
        out_weight,
        cotangent.reshape(share, width),
    )
    return (layer_out.reshape(cotangent.shape), grads.reshape(attn_inputs.shape))


def per_device(sizes, attn_inputs, cell_valid, window_shift, out_weight, cotangent):
    win_side = attn_inputs.shape[3]
    columns = attn_inputs.shape[1]
    tiles, tensors, clips = sizes
    heads = attn_inputs.shape[4] // HEAD_DIM
    fits = (
        clips == 2
        and tensors == 4
        and tiles >= 3
        and tiles <= 8
        and columns == 2 * win_side
        and heads % 2 == 0
        and out_weight.shape[1] % 128 == 0
    )
    if fits:
        one = functools.partial(fused, sizes, True)
        two = functools.partial(fused, sizes, False)
        operands = (attn_inputs, cell_valid, out_weight, cotangent)
    else:
        one = functools.partial(shifted, 1, win_side - 1)
        two = functools.partial(shifted, win_side - 1, 1)
        operands = (attn_inputs, cell_valid.astype(BF16), out_weight, cotangent)
    return lax.cond(window_shift[0] == 1, one, two, *operands)


def solution(mesh):
    placed = (
        P(None, "clips", None, "tiles", "tensor"),
        P("clips", None, "tiles"),
        P(),
        P("tensor", "tiles"),
        P("tensor", "clips", "tiles", None),
    )
    sizes = (mesh.shape["tiles"], mesh.shape["tensor"], mesh.shape["clips"])
    return jax.shard_map(
        functools.partial(per_device, sizes),
        mesh=mesh,
        in_specs=placed,
        out_specs=(P("tensor", "clips", "tiles", None), P(None, "clips", None, "tiles", "tensor")),
        check_vma=False,
    )
```

```python
import functools
import math

import jax
import jax.numpy as jnp
from jax import lax
from jax.experimental import pallas as pl
from jax.experimental.pallas import tpu as pltpu
from jax.sharding import PartitionSpec as P

HEAD_DIM = 128


def from_behind(block, axis, distance):
    devices = range(lax.axis_size(axis))
    route = [((i - distance) % len(devices), i) for i in devices]
    return lax.ppermute(block, axis, route)


def window_view(source, win_side):
    col_count, frame_count, row_count, chan_count = source.shape
    blocks = source.reshape(
        col_count // win_side, win_side, frame_count, row_count // win_side, win_side, chan_count
    )
    blocks = blocks.transpose(0, 3, 1, 2, 4, 5)
    return blocks.reshape(
        col_count // win_side * (row_count // win_side),
        win_side * frame_count * win_side,
        chan_count,
    )


def window_unview(blocks, col_count, frame_count, row_count, win_side):
    chan_count = blocks.shape[-1]
    grid = blocks.reshape(
        col_count // win_side, row_count // win_side, win_side, frame_count, win_side, chan_count
    )
    grid = grid.transpose(0, 2, 3, 1, 4, 5)
    return grid.reshape(col_count, frame_count, row_count, chan_count)


def attend(query, key_win, values, region, keep_mask, att_scale):
    scores = (
        jnp.einsum("nqhd,nkhd->nhqk", query, key_win, preferred_element_type=jnp.float32)
        * att_scale
    )
    allowed = (region[:, None, :, None] == region[:, None, None, :]) & (
        keep_mask[:, None, None, :] > 0.5
    )
    scores = jnp.where(allowed, scores, -1e30)
    row_max = jnp.max(scores, axis=-1, keepdims=True)
    weights = jnp.exp(scores - row_max)
    probs = weights / jnp.sum(weights, axis=-1, keepdims=True)
    probs_low = probs.astype(jnp.bfloat16)
    attended = jnp.einsum(
        "nhqk,nkhd->nqhd", probs_low, values, preferred_element_type=jnp.float32
    ).astype(jnp.bfloat16)
    return (attended, probs, probs_low)


def attend_back(query, key_win, values, attended, probs, probs_low, grad_out, att_scale):
    row_total = jnp.sum(grad_out.astype(jnp.float32) * attended.astype(jnp.float32), axis=-1)
    grad_probs = jnp.einsum("nqhd,nkhd->nhqk", grad_out, values, preferred_element_type=jnp.float32)
    grad_scores = (probs * (grad_probs - jnp.transpose(row_total, (0, 2, 1))[..., None])).astype(
        jnp.bfloat16
    )
    grad_query = (
        jnp.einsum("nhqk,nkhd->nqhd", grad_scores, key_win, preferred_element_type=jnp.float32)
        * att_scale
    ).astype(jnp.bfloat16)
    grad_key = (
        jnp.einsum("nhqk,nqhd->nkhd", grad_scores, query, preferred_element_type=jnp.float32)
        * att_scale
    ).astype(jnp.bfloat16)
    grad_value = jnp.einsum(
        "nhqk,nqhd->nkhd", probs_low, grad_out, preferred_element_type=jnp.float32
    ).astype(jnp.bfloat16)
    return (grad_query, grad_key, grad_value)


def shifted(row_shift, col_shift, attn_inputs, valid_low, out_weight, cotangent):
    win_side = attn_inputs.shape[3]
    full_width = attn_inputs.shape[1]
    frame_count = attn_inputs.shape[2]
    chan_count = attn_inputs.shape[4]
    head_count = chan_count // HEAD_DIM
    att_scale = 1.0 / math.sqrt(HEAD_DIM)
    early = row_shift * 2 < win_side
    slot = 0 if early else win_side - 1
    step = -1 if early else 1
    tile_index = lax.axis_index("tiles")
    wraps = tile_index == (lax.axis_size("tiles") - 1 if early else 0)
    in_slot = jnp.arange(win_side) == slot

    def take(block, distance):
        band = block[..., slot : slot + 1, :]
        moved = from_behind(band, "tiles", distance)
        return jnp.where(in_slot[:, None], moved, block)

    win_inputs = jnp.roll(take(attn_inputs, step), -col_shift, axis=1)
    win_valid = jnp.roll(take(valid_low[..., None], step)[..., 0], -col_shift, axis=0)
    row_flag = (wraps & in_slot).astype(jnp.int32)
    col_flag = (jnp.arange(full_width) >= full_width - col_shift).astype(jnp.int32)
    region_grid = jnp.broadcast_to(
        2 * row_flag[None, None, :] + col_flag[:, None, None], (full_width, frame_count, win_side)
    )
    win_region = window_view(region_grid[..., None], win_side)[..., 0]
    win_keep = window_view(win_valid[..., None], win_side)[..., 0]

    def to_heads(source):
        blocks = window_view(source, win_side)
        return blocks.reshape(blocks.shape[0], blocks.shape[1], head_count, HEAD_DIM)

    def from_heads(stacked):
        blocks = stacked.reshape(stacked.shape[0], stacked.shape[1], chan_count)
        grid = window_unview(blocks, full_width, frame_count, win_side, win_side)
        return jnp.roll(grid, col_shift, axis=0)

    columns = lax.all_gather(out_weight, "tiles", axis=1, tiled=True)
    all_cotangent = lax.all_gather(cotangent, "tensor", axis=0, tiled=True)
    query = to_heads(win_inputs[0])
    key_win = to_heads(win_inputs[1])
    values = to_heads(win_inputs[2])
    attended, probs, probs_low = attend(query, key_win, values, win_region, win_keep, att_scale)
    own_attended = take(from_heads(attended), -step)
    layer_out = lax.psum_scatter(
        jnp.einsum(
            "wtsf,fd->wtsd", own_attended, columns, preferred_element_type=jnp.float32
        ).astype(jnp.bfloat16),
        "tensor",
        scatter_dimension=0,
        tiled=True,
    )
    grad_attended = jnp.einsum(
        "wtsd,fd->wtsf", all_cotangent, columns, preferred_element_type=jnp.float32
    ).astype(jnp.bfloat16)
    win_grad = jnp.roll(take(grad_attended, step), -col_shift, axis=0)
    grads = attend_back(
        query, key_win, values, attended, probs, probs_low, to_heads(win_grad), att_scale
    )
    grad_rows = jnp.stack([from_heads(grad) for grad in grads])
    return (layer_out, take(grad_rows, -step))


NT_DIMS = (((1,), (1,)), ((), ()))
TN_DIMS = (((0,), (0,)), ((), ()))
NN_DIMS = (((1,), (0,)), ((), ()))
BF16 = jnp.bfloat16
F32 = jnp.float32


def mm(left, right, dims=NN_DIMS):
    return lax.dot_general(left, right, dims, preferred_element_type=F32)


def fused_kernel(
    early, col_shift, win_side, frames, tiles, tensors, clips,
    qkv, valid, weight, cot,
    out_ref, grad_ref,
    gathered, cots, band_out, band_in, valid_in, win_qkv, att, att_out, att_in, own_att,
    probs, biases, grad_half, grad_out, grad_in, grad_win, results, res_out, res_in, parts, shares,
    w_send, w_recv, f_send, f_recv, c_send, c_recv, b_send, b_recv, r_send, r_recv,
):
    cells, chans = qkv.shape[1], qkv.shape[2]
    heads = chans // HEAD_DIM
    half_heads = heads // 2
    half = chans // 2
    cols = weight.shape[1]
    share = cot.shape[0]
    bands = cells // win_side
    win = cells // 2
    roll = col_shift * frames * win_side
    scale = 1.0 / math.sqrt(HEAD_DIM)
    slot = 0 if early else win_side - 1
    step = -1 if early else 1
    z = lax.axis_index("tiles")
    t = lax.axis_index("tensor")
    c = lax.axis_index("clips")
    wraps = z == (tiles - 1 if early else 0)

    def tile(k):
        return {"tiles": lax.rem(z + (k % tiles), tiles)}

    def tensor(k):
        return {"tensor": lax.rem(t + (k % tensors), tensors)}

    partner = {"clips": 1 - c}

    def remote(src, dst, send, recv, device):
        return pltpu.make_async_remote_copy(
            src_ref=src, dst_ref=dst, send_sem=send, recv_sem=recv,
            device_id=device, device_id_type=pl.DeviceIdType.MESH,
        )

    barrier = pltpu.get_barrier_semaphore()
    peers = [tile(k) for k in range(1, tiles)] + [tensor(k) for k in range(1, tensors)] + [partner]
    for peer in peers:
        pl.semaphore_signal(barrier, inc=1, device_id=peer, device_id_type=pl.DeviceIdType.MESH)

    picks = lax.broadcasted_iota(jnp.int32, (bands, cells), 1)
    rows = lax.broadcasted_iota(jnp.int32, (bands, cells), 0)
    pick = (picks == rows * win_side + slot).astype(BF16)
    put_rows = lax.broadcasted_iota(jnp.int32, (cells, bands), 0)
    put_cols = lax.broadcasted_iota(jnp.int32, (cells, bands), 1)
    put = (put_rows == put_cols * win_side + slot).astype(BF16)

    def take(block):
        return mm(pick, block).astype(BF16)

    def merge(own, band):
        spread = mm(put, band)
        at = lax.rem(lax.broadcasted_iota(jnp.int32, spread.shape, 0), win_side) == slot
        return jnp.where(at, spread, own.astype(F32)).astype(BF16)

    def rolled(block):
        return jnp.concatenate([block[roll:], block[:roll]], axis=0)

    def unrolled(block):
        return jnp.concatenate([block[cells - roll:], block[: cells - roll]], axis=0)

    for i in range(3):
        band_out[pl.ds(i * bands, bands), :] = take(qkv[i])
    pl.semaphore_wait(barrier, len(peers))

    started = []

    def go(copy):
        copy.start()
        started.append(copy)
        return copy

    band_copy = go(remote(band_out, band_in, b_send.at[0], b_recv.at[0], tile(step)))
    valid_copy = go(remote(valid, valid_in, b_send.at[1], b_recv.at[1], tile(step)))
    cross = go(remote(cot, cots.at[1], c_send.at[0], c_recv.at[0], {"tensor": lax.rem(t + 2, 4)}))
    sib_id = {"tensor": t + 1 - 2 * lax.rem(t, 2)}
    sib = go(remote(cot, cots.at[0], c_send.at[1], c_recv.at[1], sib_id))
    mine = pl.ds(pl.multiple_of(c * half, half), half)
    theirs = pl.ds(pl.multiple_of((1 - c) * half, half), half)
    first_at = 1 + 2 * (z // 2)
    third_at = 3 - (z + 1) // 2
    order = [first_at, 6 - first_at - third_at, third_at]
    guarded = []

    def go_if(condition, copy):
        guarded.append((condition, copy))

        @pl.when(condition)
        def _():
            copy.start()

    go_if(z < tiles - 1, remote(
        weight.at[mine, :], gathered.at[tiles - 2, mine, :], w_send.at[0], w_recv.at[tiles - 2],
        {"tiles": lax.rem(z + 1, tiles)},
    ))
    go_if(z > 0, remote(
        weight.at[mine, :], gathered.at[0, mine, :], w_send.at[1], w_recv.at[0],
        {"tiles": lax.rem(z + tiles - 1, tiles)},
    ))
    forward = {}

    def pass_on(n):
        k = order[n]
        at = k - 1
        remote(
            gathered.at[at, mine, :], gathered.at[at, mine, :], w_send.at[2 + n], w_recv.at[at],
            partner,
        ).wait_recv()
        up = lax.rem(at + tiles - 2, tiles - 1)
        down = lax.rem(at + 1, tiles - 1)
        from_below = z + k >= tiles
        go_if(from_below & (z < tiles - 1), remote(
            gathered.at[at, mine, :], gathered.at[up, mine, :],
            w_send.at[2 + n], w_recv.at[up], {"tiles": lax.rem(z + 1, tiles)},
        ))
        go_if(jnp.logical_not(from_below) & (z > 0), remote(
            gathered.at[at, mine, :], gathered.at[down, mine, :],
            w_send.at[2 + n], w_recv.at[down], {"tiles": lax.rem(z + tiles - 1, tiles)},
        ))
        forward[n] = go(remote(
            gathered.at[at, mine, :], gathered.at[at, mine, :],
            f_send.at[n], f_recv.at[n], partner,
        ))

    band_copy.wait_recv()
    valid_copy.wait_recv()
    for i in range(3):
        for h in range(heads):
            lanes = pl.ds(h * HEAD_DIM, HEAD_DIM)
            win_qkv[i, h] = rolled(merge(qkv[i, :, lanes], band_in[pl.ds(i * bands, bands), lanes]))

    lane = lax.broadcasted_iota(jnp.int32, (8, cells), 1)
    keep = jnp.where(lax.rem(lane, win_side) == slot, valid_in[...], valid[...])
    spot_q = lax.broadcasted_iota(jnp.int32, (win, win), 0)
    spot_k = lax.broadcasted_iota(jnp.int32, (win, win), 1)
    wrap_flag = jnp.where(wraps, 2, 0)
    for w in range(2):
        edge = (win_side - col_shift) * frames * win_side

        def region(spot):
            row_flag = jnp.where(lax.rem(spot, win_side) == slot, wrap_flag, 0)
            return row_flag + (jnp.where(spot >= edge, 1, 0) if w == 1 else 0)

        allowed = (region(spot_q) == region(spot_k)) & (keep[0:1, w * win : (w + 1) * win] > 0.5)
        biases[w] = jnp.where(allowed, 0.0, -1e30)

    def attend_head(h):
        for w in range(2):
            at = pl.ds(w * win, win)
            scores = mm(win_qkv[0, h, at], win_qkv[1, h, at], NT_DIMS) * scale + biases[w]
            row_max = jnp.max(scores, axis=-1, keepdims=True)
            weights = jnp.exp(scores - row_max)
            low = (weights / jnp.sum(weights, axis=-1, keepdims=True)).astype(BF16)
            probs[h, w] = low
            att[h, at] = mm(low, win_qkv[2, h, at]).astype(BF16)

    pl.loop(0, half_heads)(attend_head)
    pass_on(0)
    pl.loop(half_heads, heads)(attend_head)
    for h in range(heads):
        att_out[:, pl.ds(h * HEAD_DIM, HEAD_DIM)] = take(att[h])
    att_copy = go(remote(att_out, att_in, b_send.at[2], b_recv.at[2], tile(-step)))
    pass_on(1)

    att_copy.wait_recv()
    for h in range(heads):
        lanes = pl.ds(h * HEAD_DIM, HEAD_DIM)
        own_att[:, lanes] = unrolled(merge(att[h], att_in[:, lanes]))

    def cot_block(j, cols_at):
        return cot[:, cols_at] if j == 0 else cots[j - 1, :, cols_at]

    flip = 1 - 2 * lax.rem(t, 2)
    owners = [t, t + flip, lax.rem(t + 2, 4), lax.rem(t + flip + 2, 4)]

    def w_rows(k, at):
        return weight[at, :] if k is None else gathered[k - 1, at, :]

    def back(k, which):
        at = mine if which == 0 else theirs
        place = z if k is None else lax.rem(z + k, tiles)
        cols_at = pl.ds(pl.multiple_of(place * cols, cols), cols)
        for j in range(4):
            rows_at = pl.ds(pl.multiple_of(owners[j] * share, share), share)
            value = mm(cot_block(j, cols_at), w_rows(k, at), NT_DIMS)
            if k is None:
                grad_half[which, rows_at] = value
            else:
                grad_half[which, rows_at] = grad_half[which, rows_at] + value

    def share_copy(n, j, owner):
        return remote(
            parts.at[n, j - 1], shares.at[n, j - 1],
            r_send.at[n, j - 1], r_recv.at[n, j - 1], {"tensor": owner},
        )

    def project(n, k):
        def block(u):
            rows_at = pl.ds(pl.multiple_of(u * share, share), share)
            return mm(own_att[rows_at], w_rows(k, slice(None))).astype(BF16)

        for j in (3, 1):
            parts[n, j - 1] = block(owners[j])
            go(share_copy(n, j, owners[1]))
        parts[n, 3] = block(t)
        own = block(owners[2]).astype(F32)
        share_copy(n, 3, owners[1]).wait_recv()
        parts[n, 1] = (own + shares[n, 2].astype(F32)).astype(BF16)
        go(share_copy(n, 2, owners[2]))

    first = [c * half_heads, (1 - c) * half_heads]
    grad_copies = {}

    def send_grad(which):
        grad_out[which] = take(grad_half[which].astype(BF16))
        grad_copies[which] = go(remote(
            grad_out.at[which], grad_in.at[which],
            b_send.at[3 + which], b_recv.at[3 + which], tile(step),
        ))

    result_copies = {}

    def attention_back(which):
        grad_copies[which].wait_recv()
        for j in range(half_heads):
            lanes = pl.ds(j * HEAD_DIM, HEAD_DIM)
            grad_win[which, j] = rolled(
                merge(grad_half[which, :, lanes].astype(BF16), grad_in[which, :, lanes])
            )

        @pl.loop(0, half_heads)
        def _(j):
            h = first[which] + j
            for w in range(2):
                at = pl.ds(w * win, win)
                grad = grad_win[which, j, at]
                low = probs[h, w]
                total = jnp.sum(
                    grad.astype(F32) * att[h, at].astype(F32), axis=-1, keepdims=True
                )
                grad_probs = mm(grad, win_qkv[2, h, at], NT_DIMS)
                grad_scores = (low.astype(F32) * (grad_probs - total)).astype(BF16)
                results[which, 0, j, at] = (mm(grad_scores, win_qkv[1, h, at]) * scale).astype(BF16)
                results[which, 1, j, at] = (
                    mm(grad_scores, win_qkv[0, h, at], TN_DIMS) * scale
                ).astype(BF16)
                results[which, 2, j, at] = mm(low, grad, TN_DIMS).astype(BF16)

        for i in range(3):
            for j in range(half_heads):
                res_out[which, i, :, pl.ds(j * HEAD_DIM, HEAD_DIM)] = take(results[which, i, j])
        result_copies[which] = go(remote(
            res_out.at[which], res_in.at[which],
            b_send.at[5 + which], b_recv.at[5 + which], tile(-step),
        ))

    def finish(which):
        result_copies[which].wait_recv()
        for i in range(3):
            for j in range(half_heads):
                lanes = pl.ds(pl.multiple_of((first[which] + j) * HEAD_DIM, HEAD_DIM), HEAD_DIM)
                own = unrolled(merge(
                    results[which, i, j], res_in[which, i, :, pl.ds(j * HEAD_DIM, HEAD_DIM)]
                ))
                grad_ref[i, :, lanes] = own

    project(0, None)
    cross.wait_recv()
    third = go(remote(cots.at[1], cots.at[2], c_send.at[2], c_recv.at[2], sib_id))
    sib.wait_recv()
    third.wait_recv()
    back(None, 0)
    back(None, 1)
    pass_on(2)
    for n in range(3):
        back(order[n], 0)
    send_grad(0)
    for n in range(3):
        forward[n].wait_recv()
        back(order[n], 1)
        if n == 2:
            send_grad(1)
        project(n + 1, order[n])
        if n == 0:
            attention_back(0)
    attention_back(1)
    for n in range(tiles):
        place = z if n == 0 else lax.rem(z + order[n - 1], tiles)
        cols_at = pl.ds(pl.multiple_of(place * cols, cols), cols)
        total = parts[n, 3].astype(F32)
        for j in (1, 2):
            share_copy(n, j, owners[j]).wait_recv()
            total = total + shares[n, j - 1].astype(F32)
        out_ref[:, cols_at] = total.astype(BF16)
    finish(0)
    finish(1)
    for copy in started:
        copy.wait_send()

    def settle(copy):
        def done():
            copy.wait_send()

        return done

    for condition, copy in guarded:
        pl.when(condition)(settle(copy))


def fused(sizes, early, attn_inputs, cell_valid, out_weight, cotangent):
    tiles, tensors, clips = sizes
    _, columns, frames, win_side, chans = attn_inputs.shape
    col_shift = win_side - 1 if early else 1
    cells = columns * frames * win_side
    heads, half = chans // HEAD_DIM, chans // 2
    bands, win = cells // win_side, cells // 2
    share = cells // tensors
    cols = out_weight.shape[1]
    width = cotangent.shape[-1]
    flat_valid = jnp.roll(cell_valid, -col_shift, axis=0).astype(F32).reshape(1, cells)
    vmem = pltpu.VMEM
    dma = pltpu.SemaphoreType.DMA
    in_vmem = pl.BlockSpec(memory_space=pltpu.VMEM)
    layer_out, grads = pl.pallas_call(
        functools.partial(
            fused_kernel, early, col_shift, win_side, frames, tiles, tensors, clips
        ),
        out_shape=(
            jax.ShapeDtypeStruct((share, width), BF16),
            jax.ShapeDtypeStruct((3, cells, chans), BF16),
        ),
        in_specs=[in_vmem] * 4,
        out_specs=(in_vmem, in_vmem),
        scratch_shapes=[
            vmem((tiles - 1, chans, cols), BF16),
            vmem((3, share, width), BF16),
            vmem((3 * bands, chans), BF16),
            vmem((3 * bands, chans), BF16),
            vmem((8, cells), F32),
            vmem((3, heads, cells, HEAD_DIM), BF16),
            vmem((heads, cells, HEAD_DIM), BF16),
            vmem((bands, chans), BF16),
            vmem((bands, chans), BF16),
            vmem((cells, chans), BF16),
            vmem((heads, 2, win, win), BF16),
            vmem((2, win, win), F32),
            vmem((2, cells, half), F32),
            vmem((2, bands, half), BF16),
            vmem((2, bands, half), BF16),
            vmem((2, heads // 2, cells, HEAD_DIM), BF16),
            vmem((2, 3, heads // 2, cells, HEAD_DIM), BF16),
            vmem((2, 3, bands, half), BF16),
            vmem((2, 3, bands, half), BF16),
            vmem((tiles, 4, share, cols), BF16),
            vmem((tiles, 3, share, cols), BF16),
            dma((tiles + 1,)), dma((tiles - 1,)), dma((tiles - 1,)), dma((tiles - 1,)),
            dma((3,)), dma((3,)), dma((7,)), dma((7,)), dma((tiles, 3)), dma((tiles, 3)),
        ],
        compiler_params=pltpu.CompilerParams(
            collective_id=0 if early else 1,
            has_side_effects=True,
            vmem_limit_bytes=56 * 2**20,
        ),
        name="fused_early" if early else "fused_late",
    )(
        attn_inputs.reshape(3, cells, chans),
        jnp.broadcast_to(flat_valid, (8, cells)),
        out_weight,
        cotangent.reshape(share, width),
    )
    return (layer_out.reshape(cotangent.shape), grads.reshape(attn_inputs.shape))


def per_device(sizes, attn_inputs, cell_valid, window_shift, out_weight, cotangent):
    win_side = attn_inputs.shape[3]
    columns = attn_inputs.shape[1]
    tiles, tensors, clips = sizes
    heads = attn_inputs.shape[4] // HEAD_DIM
    fits = (
        clips == 2
        and tensors == 4
        and tiles == 4
        and columns == 2 * win_side
        and heads % 2 == 0
        and out_weight.shape[1] % 128 == 0
    )
    if fits:
        one = functools.partial(fused, sizes, True)
        two = functools.partial(fused, sizes, False)
        operands = (attn_inputs, cell_valid, out_weight, cotangent)
    else:
        one = functools.partial(shifted, 1, win_side - 1)
        two = functools.partial(shifted, win_side - 1, 1)
        operands = (attn_inputs, cell_valid.astype(BF16), out_weight, cotangent)
    return lax.cond(window_shift[0] == 1, one, two, *operands)


def solution(mesh):
    placed = (
        P(None, "clips", None, "tiles", "tensor"),
        P("clips", None, "tiles"),
        P(),
        P("tensor", "tiles"),
        P("tensor", "clips", "tiles", None),
    )
    sizes = (mesh.shape["tiles"], mesh.shape["tensor"], mesh.shape["clips"])
    return jax.shard_map(
        functools.partial(per_device, sizes),
        mesh=mesh,
        in_specs=placed,
        out_specs=(P("tensor", "clips", "tiles", None), P(None, "clips", None, "tiles", "tensor")),
        check_vma=False,
    )
```
